32 devices in a mesh: groups: 2 (over y), curve: 16 (over z, x, core).
Axes of the slice: x: 2, y: 2, z: 4, core: 2. Of those that a mesh axis runs over, the one named last changes fastest.
Arguments:
- tracer_mass: float32 [9216, 200], P(('groups', 'curve')), parts along dimension 0, may hold values from 0.1 to 10
- send_ids: int32 [128, 32], P(('groups', 'curve')), parts along dimension 0, may hold values from 0 to 31, as said below
- send_counts: int32 [128], P(('groups', 'curve')), parts along dimension 0, may hold values from 1 to 32, as said below
- sources: int32 [9216, 4], P(('groups', 'curve')), parts along dimension 0, may hold values from 0 to 1439
- fractions: float32 [9216, 4], P(('groups', 'curve')), parts along dimension 0, may hold values from 0.02 to 0.25
- moments: float32 [2, 9216, 4], P(None, ('groups', 'curve')), parts along dimension 1, may hold values from -0.5 to 0.5
Outputs:
- new_mass: float32 [9216, 200], P(('groups', 'curve')), parts along dimension 0
The draws below stay inside these ranges and needn't reach their ends.
There are 2 independent parts, one for each index of `groups`. The reference program is written for one: setup_inputs(seed, part) draws one part's arguments, and reference() takes and returns one part's arrays. A program takes and returns all parts, laid end to end along the dimension named above; each array names one. Nothing has to cross between parts.
Inputs may be any that keep to these rules, and one draw needn't show every extreme that they name: `send_ids`: each row holds distinct local element indices of the owning device. `send_counts`: slots below the count are live; in every draw some lists reach 32. `sources`: indices into the device's own extended cells.
All inputs are finite; a program needn't handle non-finite values.
Results may differ from the reference program's by a relative error of at most 0.0001.
Values sent between devices are 32-bit elements; how exact they have to be, the bound alone decides.
A program may use at most 64 MiB of HBM per device.

```python
import math
import jax
import jax.numpy as jnp
from jax import lax

E_DEV = 32
SEND = 32
PIECES = 4
LT = 200
LISTS = 64
CELLS_ALL = 4608
EXT_CELLS = 1440
N_CURVE = 16


def draw_send_ids(key, part):
    scores = jax.random.randint(jax.random.fold_in(key, 11), (LISTS, E_DEV), 0, 2 ** 20) * E_DEV + jnp.arange(E_DEV, dtype=jnp.int32)[None, :]
    order = jnp.argsort(scores, axis=1, stable=True)
    return order[:, :SEND].astype(jnp.int32)


def draw_send_counts(key, part):
    counts = jax.random.randint(jax.random.fold_in(key, 23), (LISTS,), max(1, SEND // 8), SEND + 1)
    forced = jnp.arange(LISTS, dtype=jnp.int32) % 5 == 0
    return jnp.where(forced, SEND, counts).astype(jnp.int32)


def place_ends(entries, key, low, largest):
    extent = entries.shape
    spot = [jax.random.randint(jax.random.fold_in(key, axis), (), 0, extent[axis]) for axis in range(len(extent))]
    entries = entries.at[tuple(spot)].set(low)
    longest = extent.index(max(extent))
    spot[longest] = (spot[longest] + 1) % extent[longest]
    return entries.at[tuple(spot)].set(largest)


def level_of(rng, shape, split, smallest, high):
    loudness = 1.0
    for position, parts in split:
        steps = jax.random.uniform(jax.random.fold_in(jax.random.fold_in(rng, 6), position), (parts,), jnp.float32, smallest / len(split), high / len(split))
        loudness = loudness * jnp.repeat(jnp.exp(steps), shape[position] // parts).reshape((-1,) + (1,) * (len(shape) - 1 - position))
    return loudness


def setup_inputs(seed: int = 0, part: int = 0) -> dict:
    arg_keys = jax.random.split(jax.random.key(seed), 7)
    part_keys = jax.random.split(jax.random.fold_in(arg_keys[6], part), 7)
    tracer_mass = jnp.clip(jnp.exp(math.log(10.0) - 4.6051702 * jax.random.uniform(part_keys[0], (CELLS_ALL, LT), jnp.float32) ** level_of(part_keys[0], (CELLS_ALL, LT), ((0, 16),), -0.2, 0.2)), 0.1, 10.0)
    send_ids = draw_send_ids(jax.random.fold_in(jax.random.fold_in(arg_keys[6], part), 71), part)
    send_counts = draw_send_counts(jax.random.fold_in(jax.random.fold_in(arg_keys[6], part), 71), part)
    sources = place_ends(jax.random.randint(part_keys[3], (CELLS_ALL, PIECES), 0, EXT_CELLS), jax.random.fold_in(part_keys[3], 1), 0, EXT_CELLS - 1).astype(jnp.int32)
    fractions = jnp.clip(0.02 + 0.23 * jax.random.uniform(part_keys[4], (CELLS_ALL, PIECES), jnp.float32) ** level_of(part_keys[4], (CELLS_ALL, PIECES), ((0, 16),), -0.2, 0.2), 0.02, 0.25)
    moments = jnp.clip(jax.random.uniform(part_keys[5], (2, CELLS_ALL, PIECES), jnp.float32, -0.5, 0.5) * level_of(part_keys[5], (2, CELLS_ALL, PIECES), ((1, 16),), -0.4, 0.0), -0.5, 0.5)
    return dict(tracer_mass=tracer_mass, send_ids=send_ids, send_counts=send_counts, sources=sources, fractions=fractions, moments=moments)


OFFSETS = (1, 2, -1, -2)


def differ(cells, axis):
    first = jnp.take(cells, 0, axis=axis)
    middle = jnp.take(cells, 1, axis=axis)
    last = jnp.take(cells, 2, axis=axis)
    return jnp.stack([middle - first, 0.5 * (last - first), last - middle], axis=axis)


def transport(extended, sources_dev, fraction_dev, moment_x, moment_y):
    width = extended.shape[-1]
    total_cells = extended.shape[0] * 9
    cells = extended.reshape(-1, 3, 3, width)
    slope_x = differ(cells, 2).reshape(-1, 9, width)
    slope_y = differ(cells, 1).reshape(-1, 9, width)
    table = jnp.stack([extended, slope_x, slope_y], axis=2).reshape(total_cells, 3, width)
    inflow = jnp.zeros((sources_dev.shape[0], width), jnp.float32)
    outflow = jnp.zeros((total_cells, width), jnp.float32)
    for column in range(sources_dev.shape[1]):
        picked = table[sources_dev[:, column]]
        flux = fraction_dev[:, column, None] * (picked[:, 0] + moment_x[:, column, None] * picked[:, 1] + moment_y[:, column, None] * picked[:, 2])
        inflow = inflow + flux
        outflow = outflow + jax.ops.segment_sum(flux, sources_dev[:, column], num_segments=total_cells)
    return inflow, outflow


def reference(tracer_mass, send_ids, send_counts, sources, fractions, moments):
    mass = tracer_mass.reshape(N_CURVE, E_DEV, 9, LT)
    id_lists = send_ids.reshape(N_CURVE, 4, SEND).astype(jnp.int32)
    counts = send_counts.reshape(N_CURVE, 4)
    live = (jnp.arange(SEND, dtype=jnp.int32)[None, None, :] < counts[:, :, None]).astype(jnp.float32)
    packed = jax.vmap(lambda block, idx: block[idx])(mass, id_lists) * live[..., None, None]
    received = jnp.stack([jnp.roll(packed[:, slot], OFFSETS[slot], axis=0) for slot in range(4)], axis=1)
    extended = jnp.concatenate([mass, received.reshape(N_CURVE, 4 * SEND, 9, LT)], axis=1)
    src_all = sources.reshape(N_CURVE, 9 * E_DEV, PIECES).astype(jnp.int32)
    frac_all = fractions.reshape(N_CURVE, 9 * E_DEV, PIECES)
    mom_x = moments[0].reshape(N_CURVE, 9 * E_DEV, PIECES)
    mom_y = moments[1].reshape(N_CURVE, 9 * E_DEV, PIECES)

    def per_device(items):
        return transport(*items)

    inflow, outflow = lax.map(per_device, (extended, src_all, frac_all, mom_x, mom_y))
    returned = outflow[:, 9 * E_DEV:].reshape(N_CURVE, 4, SEND, 9, LT)
    back = jnp.stack([jnp.roll(returned[:, slot], -OFFSETS[slot], axis=0) for slot in range(4)], axis=1)
    back = back * live[..., None, None]
    own = outflow[:, :9 * E_DEV].reshape(N_CURVE, E_DEV, 9, LT)
    own = jax.vmap(lambda block, idx, extra: block.at[idx.reshape(-1)].add(extra.reshape(-1, 9, LT)))(own, id_lists, back)
    result = mass + inflow.reshape(N_CURVE, E_DEV, 9, LT) - own
    return result.reshape(CELLS_ALL, LT)
```

```python
import functools

import jax
import jax.numpy as jnp
from jax import lax
from jax.experimental import pallas as pl
from jax.experimental.pallas import tpu as pltpu
from jax.sharding import PartitionSpec as P

OFFSETS = (1, 2, -1, -2)
ORDER = (1, 3, 0, 2)
LANES = 128
CHUNK = 32
F32 = jnp.float32
BF16 = jnp.bfloat16


def round_up(value, unit):
    return -(-value // unit) * unit


def iota(shape, axis):
    return lax.broadcasted_iota(jnp.int32, shape, axis)


def ninth(value):
    return lax.shift_right_logical(value * 7282, 16)


def dot(a, b):
    return jnp.dot(a, b, preferred_element_type=F32)


def split(value):
    high = value.astype(BF16)
    return high, (value - high.astype(F32)).astype(BF16)


def difference_matrix(size, cells, stride):
    row, col = iota((size, size), 0), iota((size, size), 1)
    step = row if stride == 1 else (row * 21846) >> 16
    place = step - 3 * ((step * 21846) >> 16)
    delta = col - row
    first = jnp.where(delta == stride, 1.0, jnp.where(delta == 0, -1.0, 0.0))
    middle = jnp.where(delta == stride, 0.5, jnp.where(delta == -stride, -0.5, 0.0))
    last = jnp.where(delta == 0, 1.0, jnp.where(delta == -stride, -1.0, 0.0))
    value = jnp.where(place == 0, first, jnp.where(place == 1, middle, last))
    return jnp.where((row < cells) & (col < cells), value, 0.0).astype(BF16)


def kernel(
    count, mass_hbm, ids_ref, counts_ref, src_ref, frac_ref, mom_ref, out_ref,
    own, got, enc, enc_got, coef, coef_got, rows, cols, wq, wx, wy, high, low, dx, dy,
    own_sem, mass_send, mass_recv, enc_send, enc_recv, coef_send, coef_recv,
):
    cells, width = own.shape
    lists, slots = ids_ref.shape
    pieces = src_ref.shape[0]
    size = wq.shape[1]
    own_elements = cells // 9
    block = round_up(size, 512)
    me = lax.axis_index("curve")

    def at(offset):
        return {"curve": lax.rem(me + offset + count, count)}

    local = pltpu.make_async_copy(mass_hbm, own, own_sem)
    local.start()

    barrier = pltpu.get_barrier_semaphore()
    for offset in OFFSETS:
        pl.semaphore_signal(
            barrier, inc=1, device_id=at(offset), device_id_type=pl.DeviceIdType.MESH
        )

    wide = jnp.concatenate([ids_ref[...]] * lists, axis=1)
    row, lane = iota(wide.shape, 0), iota(wide.shape, 1)
    slot = lane - row * slots
    live = jnp.zeros(wide.shape, jnp.int32)
    for o in range(lists):
        live = jnp.where(row == o, counts_ref[o], live)
    keep = (slot >= 0) & (slot < slots) & (slot < live)
    enc[...] = jnp.zeros(enc.shape, F32)
    enc[0:lists, :] = jnp.where(keep, wide + 1, 0).astype(F32)

    pl.semaphore_wait(barrier, len(OFFSETS))

    def remote(src, dst, send, recv, o, offset):
        return pltpu.make_async_remote_copy(
            src_ref=src, dst_ref=dst, send_sem=send.at[o], recv_sem=recv.at[o],
            device_id=at(offset), device_id_type=pl.DeviceIdType.MESH,
        )

    enc_copy = [
        remote(enc, enc_got.at[o], enc_send, enc_recv, o, OFFSETS[o]) for o in range(lists)
    ]
    mass_copy = [
        remote(mass_hbm, got.at[o], mass_send, mass_recv, o, OFFSETS[o]) for o in range(lists)
    ]
    coef_copy = [
        remote(coef.at[o + 1], coef_got.at[o], coef_send, coef_recv, o, -OFFSETS[o])
        for o in range(lists)
    ]
    for o in ORDER:
        enc_copy[o].start()
    for o in ORDER:
        mass_copy[o].start()

    dx[...] = difference_matrix(size, cells, 1)
    dy[...] = difference_matrix(size, cells, 3)
    rows[...] = jnp.zeros(rows.shape, F32)
    src = src_ref[...]
    element = ninth(src)
    inside = src - 9 * element
    frac = frac_ref[...]
    rows[8 : 8 + pieces, 0:cells] = frac
    rows[16 : 16 + pieces, 0:cells] = frac * mom_ref[0]
    rows[24 : 24 + pieces, 0:cells] = frac * mom_ref[1]

    for o in ORDER:
        enc_copy[o].wait_recv()
    table = jnp.zeros((1, lists * slots), F32)
    for o in range(lists):
        table = table + enc_got[o, o : o + 1, :]
    table = jnp.broadcast_to(table, (16, lists * slots)).astype(BF16)
    for k in range(pieces):
        e = element[k : k + 1, :]
        hit = iota((lists * slots, cells), 0) + own_elements == e
        found = dot(table, jnp.where(hit, 1.0, 0.0).astype(BF16))[0:1, :]
        part = jnp.ones(e.shape, jnp.int32)
        for o in range(1, lists):
            part = part + jnp.where(e >= own_elements + o * slots, 1, 0)
        moved = (block * part + inside[k : k + 1, :]).astype(F32) + 9.0 * (found - 1.0)
        rows[k : k + 1, 0:cells] = jnp.where(
            e < own_elements, src[k : k + 1, :].astype(F32), jnp.where(found > 0.5, moved, -1.0)
        )
    cols[...] = rows[...].T

    def build(o):
        lane_id = (iota((CHUNK, size), 1) + o * block).astype(F32)

        def step(i, sums):
            at_rows = pl.ds(pl.multiple_of(i * CHUNK, CHUNK), CHUNK)
            q = jnp.zeros((CHUNK, size), F32)
            x, y = q, q
            for k in range(pieces):
                hit = lane_id == cols[at_rows, k : k + 1]
                q = q + jnp.where(hit, cols[at_rows, 8 + k : 9 + k], 0.0)
                x = x + jnp.where(hit, cols[at_rows, 16 + k : 17 + k], 0.0)
                y = y + jnp.where(hit, cols[at_rows, 24 + k : 25 + k], 0.0)
            wq[at_rows, :] = q
            wx[at_rows, :] = x
            wy[at_rows, :] = y
            return tuple(
                s + v.reshape(CHUNK // 8, 8, size).sum(0) for s, v in zip(sums, (q, x, y))
            )

        zero = jnp.zeros((8, size), F32)
        sums = lax.fori_loop(0, cells // CHUNK, step, (zero, zero, zero))
        for j in range(3):
            coef[o, j : j + 1, :] = jnp.sum(sums[j], axis=0, keepdims=True)

    def fold(o):
        xh, xl = split(wx[...])
        yh, yl = split(wy[...])
        ddx, ddy = dx[...], dy[...]
        total = wq[...] + dot(xh, ddx) + dot(xl, ddx) + dot(yh, ddy) + dot(yl, ddy)
        h, l = split(total)
        high[o] = h
        low[o] = l

    def apply(o, value):
        vh, vl = split(value)
        h, l = high[o, :, 0:cells], low[o, :, 0:cells]
        return dot(h, vh) + dot(h, vl) + dot(l, vh)

    for o in range(lists):
        coef[o + 1] = jnp.zeros((8, size), F32)
        build(o + 1)
        coef_copy[o].start()
        fold(o + 1)

    build(0)
    for o in range(lists):
        coef_copy[o].wait_recv()
    diagonal = iota((cells, size), 0) == iota((cells, size), 1)
    for j, w in enumerate((wq, wx, wy)):
        total = coef[0, j : j + 1, :]
        for o in range(lists):
            total = total + coef_got[o, j : j + 1, :]
        w[...] = w[...] - jnp.where(diagonal, total, 0.0)
    fold(0)
    local.wait()
    mass = own[...]
    out_ref[...] = mass + apply(0, mass)
    for o in (2, 0, 3, 1):
        mass_copy[o].wait_recv()
        out_ref[...] += apply(o + 1, got[o])
    for o in range(lists):
        enc_copy[o].wait_send()
        mass_copy[o].wait_send()
        coef_copy[o].wait_send()


def local(mesh, tracer_mass, send_ids, send_counts, sources, fractions, moments):
    cells, width = tracer_mass.shape
    lists, slots = send_ids.shape
    size = round_up(cells, LANES)
    vmem = pl.BlockSpec(memory_space=pltpu.VMEM)
    dma = pltpu.SemaphoreType.DMA
    return pl.pallas_call(
        functools.partial(kernel, mesh.shape["curve"]),
        out_shape=jax.ShapeDtypeStruct((cells, width), F32),
        in_specs=[
            pl.BlockSpec(memory_space=pl.ANY),
            vmem,
            pl.BlockSpec(memory_space=pltpu.SMEM),
            vmem,
            vmem,
            vmem,
        ],
        out_specs=vmem,
        scratch_shapes=[
            pltpu.VMEM((cells, width), F32),
            pltpu.VMEM((lists, cells, width), F32),
            pltpu.VMEM((8, lists * slots), F32),
            pltpu.VMEM((lists, 8, lists * slots), F32),
            pltpu.VMEM((lists + 1, 8, size), F32),
            pltpu.VMEM((lists, 8, size), F32),
            pltpu.VMEM((LANES, size), F32),
            pltpu.VMEM((size, LANES), F32),
            pltpu.VMEM((cells, size), F32),
            pltpu.VMEM((cells, size), F32),
            pltpu.VMEM((cells, size), F32),
            pltpu.VMEM((lists + 1, cells, size), BF16),
            pltpu.VMEM((lists + 1, cells, size), BF16),
            pltpu.VMEM((size, size), BF16),
            pltpu.VMEM((size, size), BF16),
            dma,
        ]
        + [dma((lists,))] * 6,
        compiler_params=pltpu.CompilerParams(
            collective_id=0, has_side_effects=True, vmem_limit_bytes=40 * 2**20
        ),
        name="transport",
    )(tracer_mass, send_ids, send_counts, sources.T, fractions.T, moments.transpose(0, 2, 1))


def solution(mesh):
    placed = (
        P(("groups", "curve"), None),
        P(("groups", "curve"), None),
        P(("groups", "curve")),
        P(("groups", "curve"), None),
        P(("groups", "curve"), None),
        P(None, ("groups", "curve"), None),
    )
    return jax.shard_map(
        functools.partial(local, mesh),
        mesh=mesh, in_specs=placed, out_specs=P(("groups", "curve"), None), check_vma=False,
    )
```

```python
import functools

import jax
import jax.numpy as jnp
from jax import lax
from jax.experimental import pallas as pl
from jax.experimental.pallas import tpu as pltpu
from jax.sharding import PartitionSpec as P

OFFSETS = (1, 2, -1, -2)
ORDER = (1, 3, 0, 2)
LANES = 128
CHUNK = 32
PARTS = 3
F32 = jnp.float32
BF16 = jnp.bfloat16


def round_up(value, unit):
    return -(-value // unit) * unit


def iota(shape, axis):
    return lax.broadcasted_iota(jnp.int32, shape, axis)


def ninth(value):
    return lax.shift_right_logical(value * 7282, 16)


def dot(a, b):
    return jnp.dot(a, b, preferred_element_type=F32)


def split(value):
    high = value.astype(BF16)
    return high, (value - high.astype(F32)).astype(BF16)


def difference_matrix(size, cells, stride):
    row, col = iota((size, size), 0), iota((size, size), 1)
    step = row if stride == 1 else (row * 21846) >> 16
    place = step - 3 * ((step * 21846) >> 16)
    delta = col - row
    first = jnp.where(delta == stride, 1.0, jnp.where(delta == 0, -1.0, 0.0))
    middle = jnp.where(delta == stride, 0.5, jnp.where(delta == -stride, -0.5, 0.0))
    last = jnp.where(delta == 0, 1.0, jnp.where(delta == -stride, -1.0, 0.0))
    value = jnp.where(place == 0, first, jnp.where(place == 1, middle, last))
    return jnp.where((row < cells) & (col < cells), value, 0.0).astype(BF16)


def kernel(
    count, mass_hbm, ids_hbm, counts_hbm, src_hbm, frac_hbm, mom_hbm, out_ref,
    own, ids_ref, counts_ref, src_ref, frac_ref, mom_ref,
    got, enc, enc_got, coef, coef_got, rows, cols, wq, wx, wy, high, low, dx, dy, sx, sy,
    in_sem, mass_send, mass_recv, enc_send, enc_recv, coef_send, coef_recv,
):
    cells, width = own.shape
    lists, slots = ids_ref.shape
    pieces = src_ref.shape[0]
    size = wq.shape[1]
    own_elements = cells // 9
    block = round_up(size, 512)
    me = lax.axis_index("curve")

    def at(offset):
        return {"curve": lax.rem(me + offset + count, count)}

    core = lax.rem(me, 2)
    odd = lax.rem(lax.div(me, 2), 2)
    sign = 1 - 2 * odd

    barrier = pltpu.get_barrier_semaphore()
    for offset in OFFSETS + (4, -4):
        pl.semaphore_signal(
            barrier, inc=1, device_id=at(offset), device_id_type=pl.DeviceIdType.MESH
        )

    inputs = [
        pltpu.make_async_copy(a, b, in_sem.at[j])
        for j, (a, b) in enumerate((
            (ids_hbm, ids_ref), (counts_hbm, counts_ref), (src_hbm, src_ref),
            (frac_hbm, frac_ref), (mom_hbm, mom_ref), (mass_hbm, own),
        ))
    ]
    for copy in inputs:
        copy.start()
    inputs[0].wait()
    inputs[1].wait()

    wide = jnp.concatenate([ids_ref[...]] * lists, axis=1)
    row, lane = iota(wide.shape, 0), iota(wide.shape, 1)
    slot = lane - row * slots
    live = jnp.zeros(wide.shape, jnp.int32)
    for o in range(lists):
        live = jnp.where(row == o, counts_ref[o], live)
    keep = (slot >= 0) & (slot < slots) & (slot < live)
    enc[...] = jnp.zeros(enc.shape, F32)
    enc[0:lists, :] = jnp.where(keep, wide + 1, 0).astype(F32)

    pl.semaphore_wait(barrier, len(OFFSETS) + 2)

    def remote(src, dst, send, recv, o, offset):
        return pltpu.make_async_remote_copy(
            src_ref=src, dst_ref=dst, send_sem=send.at[o], recv_sem=recv.at[o],
            device_id=at(offset), device_id_type=pl.DeviceIdType.MESH,
        )

    enc_copy = [
        remote(enc, enc_got.at[o], enc_send, enc_recv, o, OFFSETS[o]) for o in range(lists)
    ]
    depth = cells // PARTS

    def pass_on(slot, src, offset):
        return [
            remote(
                src.at[pl.ds(j * depth, depth)], got.at[slot, pl.ds(j * depth, depth)],
                mass_send, mass_recv, slot * PARTS + j, offset,
            )
            for j in range(PARTS)
        ]

    shared = lax.rem(core + odd, 2)
    near = pass_on(0, mass_hbm, 2 * sign)
    far = pass_on(1, got.at[0], 4 * sign)
    sibling = pass_on(2, mass_hbm, 1 - 2 * core)
    share = pass_on(3, got.at[shared], 1 - 2 * core)
    coef_copy = [
        remote(coef.at[o + 1], coef_got.at[o], coef_send, coef_recv, o, -OFFSETS[o])
        for o in range(lists)
    ]
    for o in ORDER:
        enc_copy[o].start()
    for copy in near + sibling:
        copy.start()

    def forward(j):
        near[j].wait_recv()
        far[j].start()

    def hand_over(j):
        far[j].wait_recv()
        share[j].start()

    dx[...] = difference_matrix(size, cells, 1)
    dy[...] = difference_matrix(size, cells, 3)
    rows[...] = jnp.zeros(rows.shape, F32)
    for copy in inputs[2:5]:
        copy.wait()
    src = src_ref[...]
    element = ninth(src)
    inside = src - 9 * element
    frac = frac_ref[...]
    rows[8 : 8 + pieces, 0:cells] = frac
    rows[16 : 16 + pieces, 0:cells] = frac * mom_ref[0]
    rows[24 : 24 + pieces, 0:cells] = frac * mom_ref[1]

    for o in ORDER:
        enc_copy[o].wait_recv()
    table = jnp.zeros((1, lists * slots), F32)
    for o in range(lists):
        table = table + enc_got[o, o : o + 1, :]
    table = jnp.broadcast_to(table, (16, lists * slots)).astype(BF16)
    for k in range(pieces):
        e = element[k : k + 1, :]
        hit = iota((lists * slots, cells), 0) + own_elements == e
        found = dot(table, jnp.where(hit, 1.0, 0.0).astype(BF16))[0:1, :]
        part = jnp.ones(e.shape, jnp.int32)
        for o in range(1, lists):
            part = part + jnp.where(e >= own_elements + o * slots, 1, 0)
        moved = (block * part + inside[k : k + 1, :]).astype(F32) + 9.0 * (found - 1.0)
        rows[k : k + 1, 0:cells] = jnp.where(
            e < own_elements, src[k : k + 1, :].astype(F32), jnp.where(found > 0.5, moved, -1.0)
        )
    cols[...] = rows[...].T

    def build(o):
        lane_id = (iota((CHUNK, size), 1) + o * block).astype(F32)

        def step(i, sums):
            at_rows = pl.ds(pl.multiple_of(i * CHUNK, CHUNK), CHUNK)
            q = jnp.zeros((CHUNK, size), F32)
            x, y = q, q
            for k in range(pieces):
                hit = lane_id == cols[at_rows, k : k + 1]
                q = q + jnp.where(hit, cols[at_rows, 8 + k : 9 + k], 0.0)
                x = x + jnp.where(hit, cols[at_rows, 16 + k : 17 + k], 0.0)
                y = y + jnp.where(hit, cols[at_rows, 24 + k : 25 + k], 0.0)
            wq[at_rows, :] = q
            wx[at_rows, :] = x
            wy[at_rows, :] = y
            return tuple(
                s + v.reshape(CHUNK // 8, 8, size).sum(0) for s, v in zip(sums, (q, x, y))
            )

        zero = jnp.zeros((8, size), F32)
        sums = lax.fori_loop(0, cells // CHUNK, step, (zero, zero, zero))
        for j in range(3):
            coef[o, j : j + 1, :] = jnp.sum(sums[j], axis=0, keepdims=True)

    def fold(o):
        xh, xl = split(wx[...])
        yh, yl = split(wy[...])
        ddx, ddy = dx[...], dy[...]
        total = wq[...] + dot(xh, ddx) + dot(xl, ddx) + dot(yh, ddy) + dot(yl, ddy)
        h, l = split(total)
        high[o] = h
        low[o] = l

    def apply(o, value):
        vh, vl = split(value)
        h, l = high[o, :, 0:cells], low[o, :, 0:cells]
        return dot(h, vh) + dot(h, vl) + dot(l, vh)

    for o in range(lists):
        coef[o + 1] = jnp.zeros((8, size), F32)
        build(o + 1)
        coef_copy[o].start()
        if o < PARTS:
            forward(o)
        fold(o + 1)
    hand_over(0)

    coef[0] = jnp.zeros((8, size), F32)
    build(0)
    fold(0)
    hand_over(1)
    inputs[5].wait()
    mass = own[...]
    vh, vl = split(mass)
    ddx, ddy = dx[0:cells, 0:cells], dy[0:cells, 0:cells]
    sx[...] = dot(ddx, vh) + dot(ddx, vl)
    sy[...] = dot(ddy, vh) + dot(ddy, vl)
    out_ref[...] = mass + apply(0, mass)
    hand_over(2)

    def add(copies, slot, o):
        if copies is not None:
            for copy in copies:
                copy.wait_recv()
        out_ref[...] += apply(o + 1, got[slot])

    add(sibling, 2, 2 - 2 * core)
    add(None, 0, 3 - 2 * odd)
    add(None, 1, 1 + 2 * odd)
    for o in range(lists):
        coef_copy[o].wait_recv()
    total = coef[0]
    for o in range(lists):
        total = total + coef_got[o]
    rows[0:8, :] = total
    cols[...] = rows[...].T
    out_ref[...] -= (
        cols[0:cells, 0:1] * own[...] + cols[0:cells, 1:2] * sx[...] + cols[0:cells, 2:3] * sy[...]
    )
    add(share, 3, 2 * core)
    for copy in enc_copy + near + far + sibling + share + coef_copy:
        copy.wait_send()


def local(mesh, tracer_mass, send_ids, send_counts, sources, fractions, moments):
    cells, width = tracer_mass.shape
    lists, slots = send_ids.shape
    size = round_up(cells, LANES)
    dma = pltpu.SemaphoreType.DMA
    return pl.pallas_call(
        functools.partial(kernel, mesh.shape["curve"]),
        out_shape=jax.ShapeDtypeStruct((cells, width), F32),
        in_specs=[pl.BlockSpec(memory_space=pl.ANY)] * 6,
        out_specs=pl.BlockSpec(memory_space=pltpu.VMEM),
        scratch_shapes=[
            pltpu.VMEM((cells, width), F32),
            pltpu.VMEM(send_ids.shape, jnp.int32),
            pltpu.SMEM(send_counts.shape, jnp.int32),
            pltpu.VMEM(sources.shape[::-1], jnp.int32),
            pltpu.VMEM(fractions.shape[::-1], F32),
            pltpu.VMEM((2,) + fractions.shape[::-1], F32),
            pltpu.VMEM((lists, cells, width), F32),
            pltpu.VMEM((8, lists * slots), F32),
            pltpu.VMEM((lists, 8, lists * slots), F32),
            pltpu.VMEM((lists + 1, 8, size), F32),
            pltpu.VMEM((lists, 8, size), F32),
            pltpu.VMEM((LANES, size), F32),
            pltpu.VMEM((size, LANES), F32),
            pltpu.VMEM((cells, size), F32),
            pltpu.VMEM((cells, size), F32),
            pltpu.VMEM((cells, size), F32),
            pltpu.VMEM((lists + 1, cells, size), BF16),
            pltpu.VMEM((lists + 1, cells, size), BF16),
            pltpu.VMEM((size, size), BF16),
            pltpu.VMEM((size, size), BF16),
            pltpu.VMEM((cells, width), F32),
            pltpu.VMEM((cells, width), F32),
            dma((6,)),
        ]
        + [dma((lists * PARTS,))] * 2
        + [dma((lists,))] * 4,
        compiler_params=pltpu.CompilerParams(collective_id=0, has_side_effects=True),
        name="transport",
    )(tracer_mass, send_ids, send_counts, sources.T, fractions.T, moments.transpose(0, 2, 1))


def solution(mesh):
    placed = (
        P(("groups", "curve"), None),
        P(("groups", "curve"), None),
        P(("groups", "curve")),
        P(("groups", "curve"), None),
        P(("groups", "curve"), None),
        P(None, ("groups", "curve"), None),
    )
    return jax.shard_map(
        functools.partial(local, mesh),
        mesh=mesh, in_specs=placed, out_specs=P(("groups", "curve"), None), check_vma=False,
    )
```

```python
import functools

import jax
import jax.numpy as jnp
from jax import lax
from jax.experimental import pallas as pl
from jax.experimental.pallas import tpu as pltpu
from jax.sharding import PartitionSpec as P

OFFSETS = (1, 2, -1, -2)
ORDER = (1, 3, 0, 2)
LANES = 128
CHUNK = 32
PARTS = 3
UNROLL = 3
F32 = jnp.float32
BF16 = jnp.bfloat16


def round_up(value, unit):
    return -(-value // unit) * unit


def iota(shape, axis):
    return lax.broadcasted_iota(jnp.int32, shape, axis)


def ninth(value):
    return lax.shift_right_logical(value * 7282, 16)


def dot(a, b):
    return jnp.dot(a, b, preferred_element_type=F32)


def split(value):
    high = value.astype(BF16)
    return high, (value - high.astype(F32)).astype(BF16)


def difference_matrix(size, cells, stride):
    row, col = iota((size, size), 0), iota((size, size), 1)
    step = row if stride == 1 else (row * 21846) >> 16
    place = step - 3 * ((step * 21846) >> 16)
    delta = col - row
    first = jnp.where(delta == stride, 1.0, jnp.where(delta == 0, -1.0, 0.0))
    middle = jnp.where(delta == stride, 0.5, jnp.where(delta == -stride, -0.5, 0.0))
    last = jnp.where(delta == 0, 1.0, jnp.where(delta == -stride, -1.0, 0.0))
    value = jnp.where(place == 0, first, jnp.where(place == 1, middle, last))
    return jnp.where((row < cells) & (col < cells), value, 0.0).astype(BF16)


def kernel(
    count, mass_hbm, ids_hbm, counts_hbm, src_hbm, frac_hbm, mom_hbm, out_ref,
    own, ids_ref, counts_ref, src_ref, frac_ref, mom_ref,
    got, enc, enc_got, coef, coef_got, rows, cols, wq, wx, wy, high, low, dx, dy, sx, sy,
    in_sem, mass_send, mass_recv, enc_send, enc_recv, coef_send, coef_recv,
):
    cells, width = own.shape
    lists, slots = ids_ref.shape
    pieces = src_ref.shape[0]
    size = wq.shape[1]
    own_elements = cells // 9
    block = round_up(size, 512)
    me = lax.axis_index("curve")

    def at(offset):
        return {"curve": lax.rem(me + offset + count, count)}

    core = lax.rem(me, 2)
    odd = lax.rem(lax.div(me, 2), 2)
    sign = 1 - 2 * odd

    barrier = pltpu.get_barrier_semaphore()
    for offset in OFFSETS + (4, -4):
        pl.semaphore_signal(
            barrier, inc=1, device_id=at(offset), device_id_type=pl.DeviceIdType.MESH
        )

    inputs = [
        pltpu.make_async_copy(a, b, in_sem.at[j])
        for j, (a, b) in enumerate((
            (ids_hbm, ids_ref), (counts_hbm, counts_ref), (src_hbm, src_ref),
            (frac_hbm, frac_ref), (mom_hbm, mom_ref), (mass_hbm, own),
        ))
    ]
    for copy in inputs:
        copy.start()
    inputs[0].wait()
    inputs[1].wait()

    wide = jnp.concatenate([ids_ref[...]] * lists, axis=1)
    row, lane = iota(wide.shape, 0), iota(wide.shape, 1)
    slot = lane - row * slots
    live = jnp.zeros(wide.shape, jnp.int32)
    for o in range(lists):
        live = jnp.where(row == o, counts_ref[o], live)
    keep = (slot >= 0) & (slot < slots) & (slot < live)
    enc[...] = jnp.zeros(enc.shape, F32)
    enc[0:lists, :] = jnp.where(keep, wide + 1, 0).astype(F32)

    pl.semaphore_wait(barrier, len(OFFSETS) + 2)

    def remote(src, dst, send, recv, o, offset):
        return pltpu.make_async_remote_copy(
            src_ref=src, dst_ref=dst, send_sem=send.at[o], recv_sem=recv.at[o],
            device_id=at(offset), device_id_type=pl.DeviceIdType.MESH,
        )

    enc_copy = [
        remote(enc, enc_got.at[o], enc_send, enc_recv, o, OFFSETS[o]) for o in range(lists)
    ]
    depth = cells // PARTS

    def pass_on(slot, src, offset):
        return [
            remote(
                src.at[pl.ds(j * depth, depth)], got.at[slot, pl.ds(j * depth, depth)],
                mass_send, mass_recv, slot * PARTS + j, offset,
            )
            for j in range(PARTS)
        ]

    shared = lax.rem(core + odd, 2)
    near = pass_on(0, mass_hbm, 2 * sign)
    far = pass_on(1, got.at[0], 4 * sign)
    sibling = pass_on(2, mass_hbm, 1 - 2 * core)
    share = pass_on(3, got.at[shared], 1 - 2 * core)
    coef_copy = [
        remote(coef.at[o + 1], coef_got.at[o], coef_send, coef_recv, o, -OFFSETS[o])
        for o in range(lists)
    ]
    for o in ORDER:
        enc_copy[o].start()
    for copy in near + sibling:
        copy.start()

    def forward(j):
        near[j].wait_recv()
        far[j].start()

    def hand_over(j):
        far[j].wait_recv()
        share[j].start()

    dx[...] = difference_matrix(size, cells, 1)
    dy[...] = difference_matrix(size, cells, 3)
    rows[...] = jnp.zeros(rows.shape, F32)
    for copy in inputs[2:5]:
        copy.wait()
    src = src_ref[...]
    element = ninth(src)
    inside = src - 9 * element
    frac = frac_ref[...]
    rows[8 : 8 + pieces, 0:cells] = frac
    rows[16 : 16 + pieces, 0:cells] = frac * mom_ref[0]
    rows[24 : 24 + pieces, 0:cells] = frac * mom_ref[1]

    def build(o):
        lane_id = (iota((CHUNK, size), 1) + o * block).astype(F32)

        def chunk(start, sums):
            at_rows = pl.ds(pl.multiple_of(start, CHUNK), CHUNK)
            q = jnp.zeros((CHUNK, size), F32)
            x, y = q, q
            for k in range(pieces):
                hit = lane_id == cols[at_rows, k : k + 1]
                q = q + jnp.where(hit, cols[at_rows, 8 + k : 9 + k], 0.0)
                x = x + jnp.where(hit, cols[at_rows, 16 + k : 17 + k], 0.0)
                y = y + jnp.where(hit, cols[at_rows, 24 + k : 25 + k], 0.0)
            wq[at_rows, :] = q
            wx[at_rows, :] = x
            wy[at_rows, :] = y
            return tuple(
                s + v.reshape(CHUNK // 8, 8, size).sum(0) for s, v in zip(sums, (q, x, y))
            )

        def step(i, sums):
            for j in range(UNROLL):
                sums = chunk((i * UNROLL + j) * CHUNK, sums)
            return sums

        zero = jnp.zeros((8, size), F32)
        sums = lax.fori_loop(0, cells // (CHUNK * UNROLL), step, (zero, zero, zero))
        for j in range(3):
            coef[o, j : j + 1, :] = jnp.sum(sums[j], axis=0, keepdims=True)

    def fold(o):
        xh, xl = split(wx[...])
        yh, yl = split(wy[...])
        ddx, ddy = dx[...], dy[...]
        total = wq[...] + dot(xh, ddx) + dot(xl, ddx) + dot(yh, ddy) + dot(yl, ddy)
        h, l = split(total)
        high[o] = h
        low[o] = l

    def apply(o, value):
        vh, vl = split(value)
        h, l = high[o, :, 0:cells], low[o, :, 0:cells]
        return dot(h, vh) + dot(h, vl) + dot(l, vh)

    rows[0:pieces, 0:cells] = jnp.where(element < own_elements, src, -1).astype(F32)
    cols[...] = rows[...].T
    coef[0] = jnp.zeros((8, size), F32)
    build(0)

    for o in ORDER:
        enc_copy[o].wait_recv()
    table = jnp.zeros((1, lists * slots), F32)
    for o in range(lists):
        table = table + enc_got[o, o : o + 1, :]
    table = jnp.broadcast_to(table, (16, lists * slots)).astype(BF16)
    for k in range(pieces):
        e = element[k : k + 1, :]
        hit = iota((lists * slots, cells), 0) + own_elements == e
        found = dot(table, jnp.where(hit, 1.0, 0.0).astype(BF16))[0:1, :]
        part = jnp.ones(e.shape, jnp.int32)
        for o in range(1, lists):
            part = part + jnp.where(e >= own_elements + o * slots, 1, 0)
        moved = (block * part + inside[k : k + 1, :]).astype(F32) + 9.0 * (found - 1.0)
        rows[k : k + 1, 0:cells] = jnp.where(
            e < own_elements, src[k : k + 1, :].astype(F32), jnp.where(found > 0.5, moved, -1.0)
        )
    cols[...] = rows[...].T

    forward(0)
    fold(0)
    between = (lambda: forward(1), lambda: forward(2), lambda: hand_over(0), lambda: hand_over(1))
    for o in range(lists):
        coef[o + 1] = jnp.zeros((8, size), F32)
        build(o + 1)
        coef_copy[o].start()
        between[o]()
        fold(o + 1)
    inputs[5].wait()
    mass = own[...]
    vh, vl = split(mass)
    ddx, ddy = dx[0:cells, 0:cells], dy[0:cells, 0:cells]
    sx[...] = dot(ddx, vh) + dot(ddx, vl)
    sy[...] = dot(ddy, vh) + dot(ddy, vl)
    out_ref[...] = apply(0, mass)

    def add(copies, slot, o):
        if copies is not None:
            for copy in copies:
                copy.wait_recv()
        out_ref[...] += apply(o + 1, got[slot])

    add(sibling, 2, 2 - 2 * core)
    hand_over(2)
    add(None, 0, 3 - 2 * odd)
    add(None, 1, 1 + 2 * odd)
    for o in range(lists):
        coef_copy[o].wait_recv()
    total = coef[0]
    for o in range(lists):
        total = total + coef_got[o]
    rows[0:8, :] = total
    cols[...] = rows[...].T
    out_ref[...] -= (
        cols[0:cells, 0:1] * own[...] + cols[0:cells, 1:2] * sx[...] + cols[0:cells, 2:3] * sy[...]
    )
    add(share, 3, 2 * core)
    for copy in enc_copy + near + far + sibling + share + coef_copy:
        copy.wait_send()


def local(mesh, tracer_mass, send_ids, send_counts, sources, fractions, moments):
    cells, width = tracer_mass.shape
    lists, slots = send_ids.shape
    size = round_up(cells, LANES)
    dma = pltpu.SemaphoreType.DMA
    change = pl.pallas_call(
        functools.partial(kernel, mesh.shape["curve"]),
        out_shape=jax.ShapeDtypeStruct((cells, width), F32),
        in_specs=[pl.BlockSpec(memory_space=pl.ANY)] * 6,
        out_specs=pl.BlockSpec(memory_space=pltpu.VMEM),
        scratch_shapes=[
            pltpu.VMEM((cells, width), F32),
            pltpu.VMEM(send_ids.shape, jnp.int32),
            pltpu.SMEM(send_counts.shape, jnp.int32),
            pltpu.VMEM(sources.shape[::-1], jnp.int32),
            pltpu.VMEM(fractions.shape[::-1], F32),
            pltpu.VMEM((2,) + fractions.shape[::-1], F32),
            pltpu.VMEM((lists, cells, width), F32),
            pltpu.VMEM((8, lists * slots), F32),
            pltpu.VMEM((lists, 8, lists * slots), F32),
            pltpu.VMEM((lists + 1, 8, size), F32),
            pltpu.VMEM((lists, 8, size), F32),
            pltpu.VMEM((LANES, size), F32),
            pltpu.VMEM((size, LANES), F32),
            pltpu.VMEM((cells, size), F32),
            pltpu.VMEM((cells, size), F32),
            pltpu.VMEM((cells, size), F32),
            pltpu.VMEM((lists + 1, cells, size), BF16),
            pltpu.VMEM((lists + 1, cells, size), BF16),
            pltpu.VMEM((size, size), BF16),
            pltpu.VMEM((size, size), BF16),
            pltpu.VMEM((cells, width), F32),
            pltpu.VMEM((cells, width), F32),
            dma((6,)),
        ]
        + [dma((lists * PARTS,))] * 2
        + [dma((lists,))] * 4,
        compiler_params=pltpu.CompilerParams(collective_id=0, has_side_effects=True),
        name="transport",
    )(tracer_mass, send_ids, send_counts, sources.T, fractions.T, moments.transpose(0, 2, 1))
    return tracer_mass + change


def solution(mesh):
    placed = (
        P(("groups", "curve"), None),
        P(("groups", "curve"), None),
        P(("groups", "curve")),
        P(("groups", "curve"), None),
        P(("groups", "curve"), None),
        P(None, ("groups", "curve"), None),
    )
    return jax.shard_map(
        functools.partial(local, mesh),
        mesh=mesh, in_specs=placed, out_specs=P(("groups", "curve"), None), check_vma=False,
    )
```

```python
import functools

import jax
import jax.numpy as jnp
from jax import lax
from jax.experimental import pallas as pl
from jax.experimental.pallas import tpu as pltpu
from jax.sharding import PartitionSpec as P

OFFSETS = (1, 2, -1, -2)
ORDER = (1, 3, 0, 2)
LANES = 128
CHUNK = 32
PARTS = 3
UNROLL = 3
F32 = jnp.float32
BF16 = jnp.bfloat16


def round_up(value, unit):
    return -(-value // unit) * unit


def iota(shape, axis):
    return lax.broadcasted_iota(jnp.int32, shape, axis)


def ninth(value):
    return lax.shift_right_logical(value * 7282, 16)


def dot(a, b):
    return jnp.dot(a, b, preferred_element_type=F32)


def split(value):
    high = value.astype(BF16)
    return high, (value - high.astype(F32)).astype(BF16)


def difference_matrix(size, cells, stride):
    row, col = iota((size, size), 0), iota((size, size), 1)
    step = row if stride == 1 else (row * 21846) >> 16
    place = step - 3 * ((step * 21846) >> 16)
    delta = col - row
    first = jnp.where(delta == stride, 1.0, jnp.where(delta == 0, -1.0, 0.0))
    middle = jnp.where(delta == stride, 0.5, jnp.where(delta == -stride, -0.5, 0.0))
    last = jnp.where(delta == 0, 1.0, jnp.where(delta == -stride, -1.0, 0.0))
    value = jnp.where(place == 0, first, jnp.where(place == 1, middle, last))
    return jnp.where((row < cells) & (col < cells), value, 0.0).astype(BF16)


def kernel(
    count, mass_hbm, ids_hbm, counts_hbm, src_hbm, frac_hbm, mom_hbm, out_ref,
    own, ids_ref, counts_ref, src_ref, frac_ref, mom_ref,
    got, enc, enc_got, coef, coef_got, rows, cols, wide_cols, wq, wx, wy, high, low, dx, dy, sx, sy,
    in_sem, mass_send, mass_recv, enc_send, enc_recv, coef_send, coef_recv,
):
    cells, width = own.shape
    lists, slots = ids_ref.shape
    pieces = src_ref.shape[0]
    size = wq.shape[1]
    own_elements = cells // 9
    block = round_up(size, 512)
    me = lax.axis_index("curve")

    def at(offset):
        return {"curve": lax.rem(me + offset + count, count)}

    core = lax.rem(me, 2)
    odd = lax.rem(lax.div(me, 2), 2)
    sign = 1 - 2 * odd

    barrier = pltpu.get_barrier_semaphore()
    for offset in OFFSETS + (4, -4):
        pl.semaphore_signal(
            barrier, inc=1, device_id=at(offset), device_id_type=pl.DeviceIdType.MESH
        )

    inputs = [
        pltpu.make_async_copy(a, b, in_sem.at[j])
        for j, (a, b) in enumerate((
            (ids_hbm, ids_ref), (counts_hbm, counts_ref), (src_hbm, src_ref),
            (frac_hbm, frac_ref), (mom_hbm, mom_ref), (mass_hbm, own),
        ))
    ]
    for copy in inputs:
        copy.start()
    inputs[0].wait()
    inputs[1].wait()

    wide = jnp.concatenate([ids_ref[...]] * lists, axis=1)
    row, lane = iota(wide.shape, 0), iota(wide.shape, 1)
    slot = lane - row * slots
    live = jnp.zeros(wide.shape, jnp.int32)
    for o in range(lists):
        live = jnp.where(row == o, counts_ref[o], live)
    keep = (slot >= 0) & (slot < slots) & (slot < live)
    enc[...] = jnp.zeros(enc.shape, F32)
    enc[0:lists, :] = jnp.where(keep, wide + 1, 0).astype(F32)

    pl.semaphore_wait(barrier, len(OFFSETS) + 2)

    def remote(src, dst, send, recv, o, offset):
        return pltpu.make_async_remote_copy(
            src_ref=src, dst_ref=dst, send_sem=send.at[o], recv_sem=recv.at[o],
            device_id=at(offset), device_id_type=pl.DeviceIdType.MESH,
        )

    enc_copy = [
        remote(enc, enc_got.at[o], enc_send, enc_recv, o, OFFSETS[o]) for o in range(lists)
    ]
    depth = cells // PARTS

    def pass_on(slot, src, offset):
        return [
            remote(
                src.at[pl.ds(j * depth, depth)], got.at[slot, pl.ds(j * depth, depth)],
                mass_send, mass_recv, slot * PARTS + j, offset,
            )
            for j in range(PARTS)
        ]

    shared = lax.rem(core + odd, 2)
    near = pass_on(0, mass_hbm, 2 * sign)
    far = pass_on(1, got.at[0], 4 * sign)
    sibling = pass_on(2, mass_hbm, 1 - 2 * core)
    share = pass_on(3, got.at[shared], 1 - 2 * core)
    coef_copy = [
        remote(coef.at[o + 1], coef_got.at[o], coef_send, coef_recv, o, -OFFSETS[o])
        for o in range(lists)
    ]
    for o in ORDER:
        enc_copy[o].start()
    for copy in near + sibling:
        copy.start()

    def forward(j):
        near[j].wait_recv()
        far[j].start()

    def hand_over(j):
        far[j].wait_recv()
        share[j].start()

    dx[...] = difference_matrix(size, cells, 1)
    dy[...] = difference_matrix(size, cells, 3)
    rows[...] = jnp.zeros(rows.shape, F32)
    for copy in inputs[2:5]:
        copy.wait()
    src = src_ref[...]
    element = ninth(src)
    inside = src - 9 * element
    frac = frac_ref[...]
    rows[8 : 8 + pieces, 0:cells] = frac
    rows[16 : 16 + pieces, 0:cells] = frac * mom_ref[0]
    rows[24 : 24 + pieces, 0:cells] = frac * mom_ref[1]

    def fill(kinds):
        cols[...] = rows[...].T
        for kind in kinds:
            for k in range(pieces):
                lane = 8 * kind + k
                wide_cols[kind * pieces + k] = jnp.broadcast_to(
                    cols[0:cells, lane : lane + 1], (cells, LANES)
                )

    def spread(index, at_rows):
        return jnp.concatenate([wide_cols[index, at_rows, :]] * (size // LANES), axis=1)

    def build(o):
        lane_id = (iota((CHUNK, size), 1) + o * block).astype(F32)

        def chunk(start, sums):
            at_rows = pl.ds(pl.multiple_of(start, CHUNK), CHUNK)
            q = jnp.zeros((CHUNK, size), F32)
            x, y = q, q
            for k in range(pieces):
                hit = lane_id == spread(k, at_rows)
                q = q + jnp.where(hit, spread(pieces + k, at_rows), 0.0)
                x = x + jnp.where(hit, spread(2 * pieces + k, at_rows), 0.0)
                y = y + jnp.where(hit, spread(3 * pieces + k, at_rows), 0.0)
            wq[at_rows, :] = q
            wx[at_rows, :] = x
            wy[at_rows, :] = y
            return tuple(
                s + v.reshape(CHUNK // 8, 8, size).sum(0) for s, v in zip(sums, (q, x, y))
            )

        def step(i, sums):
            for j in range(UNROLL):
                sums = chunk((i * UNROLL + j) * CHUNK, sums)
            return sums

        zero = jnp.zeros((8, size), F32)
        sums = lax.fori_loop(0, cells // (CHUNK * UNROLL), step, (zero, zero, zero))
        for j in range(3):
            coef[o, j : j + 1, :] = jnp.sum(sums[j], axis=0, keepdims=True)

    def fold(o):
        xh, xl = split(wx[...])
        yh, yl = split(wy[...])
        ddx, ddy = dx[...], dy[...]
        total = wq[...] + dot(xh, ddx) + dot(xl, ddx) + dot(yh, ddy) + dot(yl, ddy)
        h, l = split(total)
        high[o] = h
        low[o] = l

    def apply(o, value):
        vh, vl = split(value)
        h, l = high[o, :, 0:cells], low[o, :, 0:cells]
        return dot(h, vh) + dot(h, vl) + dot(l, vh)

    rows[0:pieces, 0:cells] = jnp.where(element < own_elements, src, -1).astype(F32)
    fill(range(4))
    coef[0] = jnp.zeros((8, size), F32)
    build(0)

    for o in ORDER:
        enc_copy[o].wait_recv()
    table = jnp.zeros((1, lists * slots), F32)
    for o in range(lists):
        table = table + enc_got[o, o : o + 1, :]
    table = jnp.broadcast_to(table, (16, lists * slots)).astype(BF16)
    for k in range(pieces):
        e = element[k : k + 1, :]
        hit = iota((lists * slots, cells), 0) + own_elements == e
        found = dot(table, jnp.where(hit, 1.0, 0.0).astype(BF16))[0:1, :]
        part = jnp.ones(e.shape, jnp.int32)
        for o in range(1, lists):
            part = part + jnp.where(e >= own_elements + o * slots, 1, 0)
        moved = (block * part + inside[k : k + 1, :]).astype(F32) + 9.0 * (found - 1.0)
        rows[k : k + 1, 0:cells] = jnp.where(
            e < own_elements, src[k : k + 1, :].astype(F32), jnp.where(found > 0.5, moved, -1.0)
        )
    fill(range(1))

    forward(0)
    fold(0)
    between = (lambda: forward(1), lambda: forward(2), lambda: hand_over(0), lambda: hand_over(1))
    for o in range(lists):
        coef[o + 1] = jnp.zeros((8, size), F32)
        build(o + 1)
        coef_copy[o].start()
        between[o]()
        fold(o + 1)
    inputs[5].wait()
    mass = own[...]
    vh, vl = split(mass)
    ddx, ddy = dx[0:cells, 0:cells], dy[0:cells, 0:cells]
    sx[...] = dot(ddx, vh) + dot(ddx, vl)
    sy[...] = dot(ddy, vh) + dot(ddy, vl)
    out_ref[...] = apply(0, mass)

    def add(copies, slot, o):
        if copies is not None:
            for copy in copies:
                copy.wait_recv()
        out_ref[...] += apply(o + 1, got[slot])

    add(sibling, 2, 2 - 2 * core)
    hand_over(2)
    add(None, 0, 3 - 2 * odd)
    add(None, 1, 1 + 2 * odd)
    for o in range(lists):
        coef_copy[o].wait_recv()
    total = coef[0]
    for o in range(lists):
        total = total + coef_got[o]
    rows[0:8, :] = total
    cols[...] = rows[...].T
    out_ref[...] -= (
        cols[0:cells, 0:1] * own[...] + cols[0:cells, 1:2] * sx[...] + cols[0:cells, 2:3] * sy[...]
    )
    add(share, 3, 2 * core)
    for copy in enc_copy + near + far + sibling + share + coef_copy:
        copy.wait_send()


def local(mesh, tracer_mass, send_ids, send_counts, sources, fractions, moments):
    cells, width = tracer_mass.shape
    lists, slots = send_ids.shape
    size = round_up(cells, LANES)
    dma = pltpu.SemaphoreType.DMA
    change = pl.pallas_call(
        functools.partial(kernel, mesh.shape["curve"]),
        out_shape=jax.ShapeDtypeStruct((cells, width), F32),
        in_specs=[pl.BlockSpec(memory_space=pl.ANY)] * 6,
        out_specs=pl.BlockSpec(memory_space=pltpu.VMEM),
        scratch_shapes=[
            pltpu.VMEM((cells, width), F32),
            pltpu.VMEM(send_ids.shape, jnp.int32),
            pltpu.SMEM(send_counts.shape, jnp.int32),
            pltpu.VMEM(sources.shape[::-1], jnp.int32),
            pltpu.VMEM(fractions.shape[::-1], F32),
            pltpu.VMEM((2,) + fractions.shape[::-1], F32),
            pltpu.VMEM((lists, cells, width), F32),
            pltpu.VMEM((8, lists * slots), F32),
            pltpu.VMEM((lists, 8, lists * slots), F32),
            pltpu.VMEM((lists + 1, 8, size), F32),
            pltpu.VMEM((lists, 8, size), F32),
            pltpu.VMEM((LANES, size), F32),
            pltpu.VMEM((size, LANES), F32),
            pltpu.VMEM((4 * sources.shape[1], cells, LANES), F32),
            pltpu.VMEM((cells, size), F32),
            pltpu.VMEM((cells, size), F32),
            pltpu.VMEM((cells, size), F32),
            pltpu.VMEM((lists + 1, cells, size), BF16),
            pltpu.VMEM((lists + 1, cells, size), BF16),
            pltpu.VMEM((size, size), BF16),
            pltpu.VMEM((size, size), BF16),
            pltpu.VMEM((cells, width), F32),
            pltpu.VMEM((cells, width), F32),
            dma((6,)),
        ]
        + [dma((lists * PARTS,))] * 2
        + [dma((lists,))] * 4,
        compiler_params=pltpu.CompilerParams(collective_id=0, has_side_effects=True),
        name="transport",
    )(tracer_mass, send_ids, send_counts, sources.T, fractions.T, moments.transpose(0, 2, 1))
    return tracer_mass + change


def solution(mesh):
    placed = (
        P(("groups", "curve"), None),
        P(("groups", "curve"), None),
        P(("groups", "curve")),
        P(("groups", "curve"), None),
        P(("groups", "curve"), None),
        P(None, ("groups", "curve"), None),
    )
    return jax.shard_map(
        functools.partial(local, mesh),
        mesh=mesh, in_specs=placed, out_specs=P(("groups", "curve"), None), check_vma=False,
    )
```

```python
import functools

import jax
import jax.numpy as jnp
from jax import lax
from jax.experimental import pallas as pl
from jax.experimental.pallas import tpu as pltpu
from jax.sharding import PartitionSpec as P

OFFSETS = (1, 2, -1, -2)
ORDER = (1, 3, 0, 2)
LANES = 128
CHUNK = 32
PARTS = 3
UNROLL = 3
F32 = jnp.float32
BF16 = jnp.bfloat16


def round_up(value, unit):
    return -(-value // unit) * unit


def iota(shape, axis):
    return lax.broadcasted_iota(jnp.int32, shape, axis)


def ninth(value):
    return lax.shift_right_logical(value * 7282, 16)


def dot(a, b):
    return jnp.dot(a, b, preferred_element_type=F32)


def split(value):
    high = value.astype(BF16)
    return high, (value - high.astype(F32)).astype(BF16)


def difference_matrix(size, cells, stride):
    row, col = iota((size, size), 0), iota((size, size), 1)
    step = row if stride == 1 else (row * 21846) >> 16
    place = step - 3 * ((step * 21846) >> 16)
    delta = col - row
    first = jnp.where(delta == stride, 1.0, jnp.where(delta == 0, -1.0, 0.0))
    middle = jnp.where(delta == stride, 0.5, jnp.where(delta == -stride, -0.5, 0.0))
    last = jnp.where(delta == 0, 1.0, jnp.where(delta == -stride, -1.0, 0.0))
    value = jnp.where(place == 0, first, jnp.where(place == 1, middle, last))
    return jnp.where((row < cells) & (col < cells), value, 0.0).astype(BF16)


def kernel(
    count, mass_hbm, ids_hbm, counts_hbm, src_hbm, frac_hbm, mom_hbm, out_ref,
    own, ids_ref, counts_ref, src_ref, frac_ref, mom_ref,
    got, enc, enc_got, coef, coef_got, rows, cols, wide_cols, wq, wx, wy, high, low, dx, dy, sx, sy,
    in_sem, mass_send, mass_recv, enc_send, enc_recv, coef_send, coef_recv,
):
    cells, width = own.shape
    lists, slots = ids_ref.shape
    pieces = src_ref.shape[0]
    size = wq.shape[1]
    own_elements = cells // 9
    block = round_up(size, 512)
    me = lax.axis_index("curve")

    def at(offset):
        return {"curve": lax.rem(me + offset + count, count)}

    core = lax.rem(me, 2)
    odd = lax.rem(lax.div(me, 2), 2)
    sign = 1 - 2 * odd

    barrier = pltpu.get_barrier_semaphore()
    for offset in OFFSETS + (4, -4):
        pl.semaphore_signal(
            barrier, inc=1, device_id=at(offset), device_id_type=pl.DeviceIdType.MESH
        )

    inputs = [
        pltpu.make_async_copy(a, b, in_sem.at[j])
        for j, (a, b) in enumerate((
            (ids_hbm, ids_ref), (counts_hbm, counts_ref), (src_hbm, src_ref),
            (frac_hbm, frac_ref), (mom_hbm, mom_ref), (mass_hbm, own),
        ))
    ]
    for copy in inputs:
        copy.start()
    inputs[0].wait()
    inputs[1].wait()

    wide = jnp.concatenate([ids_ref[...]] * lists, axis=1)
    row, lane = iota(wide.shape, 0), iota(wide.shape, 1)
    slot = lane - row * slots
    live = jnp.zeros(wide.shape, jnp.int32)
    for o in range(lists):
        live = jnp.where(row == o, counts_ref[o], live)
    keep = (slot >= 0) & (slot < slots) & (slot < live)
    enc[...] = jnp.zeros(enc.shape, F32)
    enc[0:lists, :] = jnp.where(keep, wide + 1, 0).astype(F32)

    pl.semaphore_wait(barrier, len(OFFSETS) + 2)

    def remote(src, dst, send, recv, o, offset):
        return pltpu.make_async_remote_copy(
            src_ref=src, dst_ref=dst, send_sem=send.at[o], recv_sem=recv.at[o],
            device_id=at(offset), device_id_type=pl.DeviceIdType.MESH,
        )

    enc_copy = [
        remote(enc, enc_got.at[o], enc_send, enc_recv, o, OFFSETS[o]) for o in range(lists)
    ]
    depth = cells // PARTS

    def pass_on(slot, src, offset):
        return [
            remote(
                src.at[pl.ds(j * depth, depth)], got.at[slot, pl.ds(j * depth, depth)],
                mass_send, mass_recv, slot * PARTS + j, offset,
            )
            for j in range(PARTS)
        ]

    shared = lax.rem(core + odd, 2)
    near = pass_on(0, mass_hbm, 2 * sign)
    far = pass_on(1, got.at[0], 4 * sign)
    sibling = pass_on(2, mass_hbm, 1 - 2 * core)
    share = pass_on(3, got.at[shared], 1 - 2 * core)
    coef_copy = [
        remote(coef.at[o + 1], coef_got.at[o], coef_send, coef_recv, o, -OFFSETS[o])
        for o in range(lists)
    ]
    for o in ORDER:
        enc_copy[o].start()
    for copy in near + sibling:
        copy.start()

    def forward(j):
        near[j].wait_recv()
        far[j].start()

    def hand_over(j):
        far[j].wait_recv()
        share[j].start()

    dx[...] = difference_matrix(size, cells, 1)
    dy[...] = difference_matrix(size, cells, 3)
    rows[...] = jnp.zeros(rows.shape, F32)
    for copy in inputs[2:5]:
        copy.wait()
    src = src_ref[...]
    element = ninth(src)
    inside = src - 9 * element
    frac = frac_ref[...]
    rows[8 : 8 + pieces, 0:cells] = frac
    rows[16 : 16 + pieces, 0:cells] = frac * mom_ref[0]
    rows[24 : 24 + pieces, 0:cells] = frac * mom_ref[1]

    def fill(kinds):
        cols[...] = rows[...].T
        for kind in kinds:
            for k in range(pieces):
                lane = 8 * kind + k
                wide_cols[kind * pieces + k] = jnp.broadcast_to(
                    cols[0:cells, lane : lane + 1], (cells, LANES)
                )

    def spread(index, at_rows):
        return jnp.concatenate([wide_cols[index, at_rows, :]] * (size // LANES), axis=1)

    def build(o):
        lane_id = (iota((CHUNK, size), 1) + o * block).astype(F32)

        def chunk(start, sums):
            at_rows = pl.ds(pl.multiple_of(start, CHUNK), CHUNK)
            q = jnp.zeros((CHUNK, size), F32)
            x, y = q, q
            for k in range(pieces):
                hit = lane_id == spread(k, at_rows)
                q = q + jnp.where(hit, spread(pieces + k, at_rows), 0.0)
                x = x + jnp.where(hit, spread(2 * pieces + k, at_rows), 0.0)
                y = y + jnp.where(hit, spread(3 * pieces + k, at_rows), 0.0)
            wq[at_rows, :] = q
            wx[at_rows, :] = x
            wy[at_rows, :] = y
            return tuple(
                s + v.reshape(CHUNK // 8, 8, size).sum(0) for s, v in zip(sums, (q, x, y))
            )

        def step(i, sums):
            for j in range(UNROLL):
                sums = chunk((i * UNROLL + j) * CHUNK, sums)
            return sums

        zero = jnp.zeros((8, size), F32)
        sums = lax.fori_loop(0, cells // (CHUNK * UNROLL), step, (zero, zero, zero))
        for j in range(3):
            coef[o, j : j + 1, :] = jnp.sum(sums[j], axis=0, keepdims=True)

    def fold(o):
        xh, xl = split(wx[...])
        yh, yl = split(wy[...])
        ddx, ddy = dx[...], dy[...]
        parts = jnp.concatenate([xh, xl, yh, yl], axis=1)
        total = wq[...] + dot(parts, jnp.concatenate([ddx, ddx, ddy, ddy], axis=0))
        h, l = split(total)
        high[o] = h
        low[o] = l

    def apply(o, value):
        vh, vl = split(value)
        h, l = high[o, :, 0:cells], low[o, :, 0:cells]
        return dot(h, vh) + dot(h, vl) + dot(l, vh)

    rows[0:pieces, 0:cells] = jnp.where(element < own_elements, src, -1).astype(F32)
    fill(range(4))
    coef[0] = jnp.zeros((8, size), F32)
    build(0)

    for o in ORDER:
        enc_copy[o].wait_recv()
    table = jnp.zeros((1, lists * slots), F32)
    for o in range(lists):
        table = table + enc_got[o, o : o + 1, :]
    table = jnp.broadcast_to(table, (16, lists * slots)).astype(BF16)
    for k in range(pieces):
        e = element[k : k + 1, :]
        hit = iota((lists * slots, cells), 0) + own_elements == e
        found = dot(table, jnp.where(hit, 1.0, 0.0).astype(BF16))[0:1, :]
        part = jnp.ones(e.shape, jnp.int32)
        for o in range(1, lists):
            part = part + jnp.where(e >= own_elements + o * slots, 1, 0)
        moved = (block * part + inside[k : k + 1, :]).astype(F32) + 9.0 * (found - 1.0)
        rows[k : k + 1, 0:cells] = jnp.where(
            e < own_elements, src[k : k + 1, :].astype(F32), jnp.where(found > 0.5, moved, -1.0)
        )
    fill(range(1))

    forward(0)
    fold(0)
    between = (lambda: forward(1), lambda: forward(2), lambda: hand_over(0), lambda: hand_over(1))
    for o in range(lists):
        coef[o + 1] = jnp.zeros((8, size), F32)
        build(o + 1)
        coef_copy[o].start()
        between[o]()
        fold(o + 1)
    inputs[5].wait()
    mass = own[...]
    vh, vl = split(mass)
    ddx, ddy = dx[0:cells, 0:cells], dy[0:cells, 0:cells]
    sx[...] = dot(ddx, vh) + dot(ddx, vl)
    sy[...] = dot(ddy, vh) + dot(ddy, vl)
    out_ref[...] = apply(0, mass)

    def add(copies, slot, o):
        if copies is not None:
            for copy in copies:
                copy.wait_recv()
        out_ref[...] += apply(o + 1, got[slot])

    add(sibling, 2, 2 - 2 * core)
    hand_over(2)
    add(None, 0, 3 - 2 * odd)
    add(None, 1, 1 + 2 * odd)
    for o in range(lists):
        coef_copy[o].wait_recv()
    total = coef[0]
    for o in range(lists):
        total = total + coef_got[o]
    rows[0:8, :] = total
    cols[...] = rows[...].T
    out_ref[...] -= (
        cols[0:cells, 0:1] * own[...] + cols[0:cells, 1:2] * sx[...] + cols[0:cells, 2:3] * sy[...]
    )
    add(share, 3, 2 * core)
    for copy in enc_copy + near + far + sibling + share + coef_copy:
        copy.wait_send()


def local(mesh, tracer_mass, send_ids, send_counts, sources, fractions, moments):
    cells, width = tracer_mass.shape
    lists, slots = send_ids.shape
    size = round_up(cells, LANES)
    dma = pltpu.SemaphoreType.DMA
    change = pl.pallas_call(
        functools.partial(kernel, mesh.shape["curve"]),
        out_shape=jax.ShapeDtypeStruct((cells, width), F32),
        in_specs=[pl.BlockSpec(memory_space=pl.ANY)] * 6,
        out_specs=pl.BlockSpec(memory_space=pltpu.VMEM),
        scratch_shapes=[
            pltpu.VMEM((cells, width), F32),
            pltpu.VMEM(send_ids.shape, jnp.int32),
            pltpu.SMEM(send_counts.shape, jnp.int32),
            pltpu.VMEM(sources.shape[::-1], jnp.int32),
            pltpu.VMEM(fractions.shape[::-1], F32),
            pltpu.VMEM((2,) + fractions.shape[::-1], F32),
            pltpu.VMEM((lists, cells, width), F32),
            pltpu.VMEM((8, lists * slots), F32),
            pltpu.VMEM((lists, 8, lists * slots), F32),
            pltpu.VMEM((lists + 1, 8, size), F32),
            pltpu.VMEM((lists, 8, size), F32),
            pltpu.VMEM((LANES, size), F32),
            pltpu.VMEM((size, LANES), F32),
            pltpu.VMEM((4 * sources.shape[1], cells, LANES), F32),
            pltpu.VMEM((cells, size), F32),
            pltpu.VMEM((cells, size), F32),
            pltpu.VMEM((cells, size), F32),
            pltpu.VMEM((lists + 1, cells, size), BF16),
            pltpu.VMEM((lists + 1, cells, size), BF16),
            pltpu.VMEM((size, size), BF16),
            pltpu.VMEM((size, size), BF16),
            pltpu.VMEM((cells, width), F32),
            pltpu.VMEM((cells, width), F32),
            dma((6,)),
        ]
        + [dma((lists * PARTS,))] * 2
        + [dma((lists,))] * 4,
        compiler_params=pltpu.CompilerParams(collective_id=0, has_side_effects=True),
        name="transport",
    )(tracer_mass, send_ids, send_counts, sources.T, fractions.T, moments.transpose(0, 2, 1))
    return tracer_mass + change


def solution(mesh):
    placed = (
        P(("groups", "curve"), None),
        P(("groups", "curve"), None),
        P(("groups", "curve")),
        P(("groups", "curve"), None),
        P(("groups", "curve"), None),
        P(None, ("groups", "curve"), None),
    )
    return jax.shard_map(
        functools.partial(local, mesh),
        mesh=mesh, in_specs=placed, out_specs=P(("groups", "curve"), None), check_vma=False,
    )
```
